256 devices in a mesh: row: 32 (over x, z), col: 8 (over y, core).
Axes of the slice: x: 4, y: 4, z: 8, core: 2. Of those that a mesh axis runs over, the one named last changes fastest.
Arguments:
- tiles: bfloat16 [320, 2048, 2048], P('row', None, 'col')
- tile_row: int32 [320], P('row'), may hold values from 0 to 1
- tile_col: int32 [320], P('row'), may hold values from 0 to 63, as said below
- tile_count: int32 [32], P('row'), may hold values from 1 to 10, as said below
- block_vectors: bfloat16 [64, 2048, 64], P('row', 'col')
Outputs:
- basis_out: float32 [64, 2048, 64], P('row', 'col')
The draws below stay inside these ranges and needn't reach their ends.
Inputs may be any that keep to these rules, and one draw needn't show every extreme that they name: Index r of row uses its first tile_count[r] slots; its other slots hold unused tiles. The most, 10, is reached on some index of row in every draw. `tile_col`: the live slots of index r of row name column blocks from 2 * (r - 4) to 2 * (r + 4) - 1, and distinct pairs of row block and column block.
All inputs are finite; a program needn't handle non-finite values.
Results may differ from the reference program's by a relative error of at most 0.0035.
Values may be sent and summed in bfloat16 or wider, within the bound.
No kernel may reach another device: no remote copies, remote signals or barrier semaphores. Data moves between devices by JAX's collectives and lax.ppermute only.
A program may use at most 64 MiB of HBM per device.

```python
import math
import jax
import jax.numpy as jnp
from jax import lax

TILE = 2048
K = 64
RB_DEV = 2
SLOTS = 10
REACH = 4
NB = 64
TILES = 320


def tile_plan(key):
    row_devices = NB // RB_DEV
    window_cols = 2 * REACH * RB_DEV
    candidates = RB_DEV * window_cols
    count_key, heavy_key, score_key = jax.random.split(jax.random.fold_in(key, 77), 3)
    counts = jax.random.randint(count_key, (row_devices,), 1, SLOTS // 2 + 2)
    heavy_row = jax.random.randint(heavy_key, (), REACH, row_devices - REACH + 1)
    counts = jnp.where(jnp.arange(row_devices) == heavy_row, SLOTS, counts).astype(jnp.int32)
    candidate = jnp.arange(candidates, dtype=jnp.int32)
    window_col = candidate % window_cols
    local_block = candidate // window_cols
    column_block = (jnp.arange(row_devices, dtype=jnp.int32)[:, None] - REACH) * RB_DEV + window_col[None, :]
    invalid = ((column_block < 0) | (column_block >= NB)).astype(jnp.int32)
    random_rank = jax.random.randint(score_key, (row_devices, candidates), 0, 65536)
    scores = invalid * (1 << 26) + random_rank * candidates + candidate[None, :]
    chosen = jnp.argsort(scores, axis=1)[:, :SLOTS]
    picked_rows = jnp.take(local_block, chosen)
    picked_cols = jnp.clip(jnp.take_along_axis(column_block, chosen, axis=1), 0, NB - 1)
    return (picked_rows.reshape(-1).astype(jnp.int32), picked_cols.reshape(-1).astype(jnp.int32), counts)


def draw_tile_row(key, part):
    shared = tile_plan(key)
    return shared[0]


def draw_tile_col(key, part):
    shared = tile_plan(key)
    return shared[1]


def draw_tile_count(key, part):
    shared = tile_plan(key)
    return shared[2]


def draw_tiles(key, part):
    key = jax.random.fold_in(key, 5)
    scale_key, value_key = jax.random.split(key)
    row_scale = jnp.exp(jax.random.uniform(scale_key, (TILES, TILE, 1), jnp.float32, 0.0, math.log(10.0)))
    values = jax.random.truncated_normal(value_key, -4.0, 4.0, (TILES, TILE, TILE), jnp.float32)
    return (values * row_scale / math.sqrt(8.0 * TILE)).astype(jnp.bfloat16)


def draw_block_vectors(key, part):
    key = jax.random.fold_in(key, 9)
    scale_key, value_key = jax.random.split(key)
    block_scale = 3.0 ** (jnp.arange(NB, dtype=jnp.float32) / max(NB - 1, 1))
    row_scale = jnp.exp(jax.random.uniform(scale_key, (NB, TILE, 1), jnp.float32, 0.0, math.log(3.0)))
    values = jax.random.truncated_normal(value_key, -4.0, 4.0, (NB, TILE, K), jnp.float32)
    return (values * row_scale * block_scale[:, None, None]).astype(jnp.bfloat16)


def setup_inputs(seed: int = 0) -> dict:
    key_list = jax.random.split(jax.random.key(seed), 6)
    tiles = draw_tiles(jax.random.fold_in(key_list[5], 71), 0)
    tile_row = draw_tile_row(jax.random.fold_in(key_list[5], 71), 0)
    tile_col = draw_tile_col(jax.random.fold_in(key_list[5], 71), 0)
    tile_count = draw_tile_count(jax.random.fold_in(key_list[5], 71), 0)
    block_vectors = draw_block_vectors(jax.random.fold_in(key_list[5], 71), 0)
    return {"tiles": tiles, "tile_row": tile_row, "tile_col": tile_col, "tile_count": tile_count, "block_vectors": block_vectors}


def apply_graph(tiles, target, tile_col, is_live, vectors):

    def add_tile(running, tile_item):
        tile_piece, row_block, col_block, live_flag = tile_item
        panel_rows = lax.dynamic_index_in_dim(vectors, col_block, 0, keepdims=False)
        product_term = jnp.dot(tile_piece.astype(jnp.float32), panel_rows.astype(jnp.float32), preferred_element_type=jnp.float32)
        product_term = jnp.where(live_flag, product_term, jnp.zeros_like(product_term))
        current = lax.dynamic_index_in_dim(running, row_block, 0, keepdims=False)
        return (lax.dynamic_update_index_in_dim(running, current + product_term, row_block, 0), None)
    start = jnp.zeros((NB, TILE, K), jnp.float32)
    running, _ = lax.scan(add_tile, start, (tiles, target, tile_col, is_live))
    return running

def reference(tiles, tile_row, tile_col, tile_count, block_vectors):
    slot_ids = jnp.arange(TILES, dtype=jnp.int32)
    is_live = slot_ids % SLOTS < jnp.repeat(tile_count, SLOTS)
    target = (slot_ids // SLOTS * RB_DEV + tile_row).astype(jnp.int32)
    column_ids = tile_col.astype(jnp.int32)
    first_power = apply_graph(tiles, target, column_ids, is_live, block_vectors)
    second_power = apply_graph(tiles, target, column_ids, is_live, first_power.astype(jnp.bfloat16))
    third_power = apply_graph(tiles, target, column_ids, is_live, second_power.astype(jnp.bfloat16))
    vectors_wide = block_vectors.astype(jnp.float32)
    spread = jnp.sum(first_power * first_power) / jnp.sum(vectors_wide * vectors_wide)
    filtered = 4.0 * third_power - 3.0 * spread * first_power
    flat_rows = filtered.reshape(NB * TILE, K)
    gram_matrix = jnp.dot(flat_rows.T.astype(jnp.float32), flat_rows.astype(jnp.float32), precision=lax.Precision.HIGHEST, preferred_element_type=jnp.float32)
    lower_factor = jnp.linalg.cholesky(gram_matrix)
    solved = jax.scipy.linalg.solve_triangular(lower_factor, flat_rows.T, lower=True)
    return (solved.T * math.sqrt(NB * TILE)).reshape(NB, TILE, K)
```

```python
import functools
import math

import jax
import jax.numpy as jnp
from jax import lax
from jax.experimental import pallas as pl
from jax.experimental.pallas import tpu as pltpu
from jax.sharding import Mesh, PartitionSpec as P

X, Z, Y, CORE = 4, 8, 4, 2
ALL = ("x", "z", "y", "core")
SLICE = 256
LANES = 128
HIGHEST = lax.Precision.HIGHEST
VMEM = pl.BlockSpec(memory_space=pltpu.VMEM)
SMEM = pl.BlockSpec(memory_space=pltpu.SMEM)


def x_neighbour_pairs():
    pairs = []
    for x in range(X):
        for z in range(Z):
            to = (x + 1) % X if z >= Z // 2 else (x - 1) % X
            for c in range(Y * CORE):
                pairs.append(((x * Z + z) * Y * CORE + c, (to * Z + z) * Y * CORE + c))
    return pairs


def window(own):
    z = lax.axis_index("z")
    other = lax.ppermute(own, ALL, x_neighbour_pairs())
    target = lax.broadcasted_iota(jnp.int32, (Z, 1, 1), 0)
    half = Z // 2
    use_other = jnp.where(z < half, target >= z + half + 1, target <= z - half)
    pieces = jnp.where(use_other, other[None], own[None])
    return lax.all_to_all(pieces, "z", 0, 0)


def apply_kernel(meta, tiles, slots, out, rhs):
    count = tiles.shape[0]
    lane = lax.broadcasted_iota(jnp.int32, (SLICE, LANES), 1)
    half = LANES // 2
    for t in range(count):
        slot, parity, block, live = (meta[1 + 4 * t + i] for i in range(4))
        vectors = slots[slot].astype(jnp.float32)
        turned = pltpu.roll(vectors, half, axis=1)
        vectors = jnp.where(parity == block, vectors, turned)
        first = block * half
        keep = (lane >= first) & (lane < first + half) & (live > 0)
        rhs[t] = jnp.where(keep, vectors, 0.0).astype(jnp.bfloat16)

    def one(y, carry):
        start = pl.multiple_of((y * CORE + meta[0]) * SLICE, SLICE)
        total = jnp.zeros((SLICE, LANES), jnp.float32)
        for t in range(count):
            total = total + jnp.dot(
                tiles[t, pl.ds(start, SLICE), :], rhs[t], preferred_element_type=jnp.float32
            )
        out[y] = total
        return carry

    lax.fori_loop(0, Y, one, 0)


def apply_half(meta, tiles, slots):
    count = tiles.shape[0]
    return pl.pallas_call(
        apply_kernel,
        out_shape=jax.ShapeDtypeStruct((Y, SLICE, LANES), jnp.float32),
        in_specs=[SMEM, VMEM, VMEM],
        out_specs=VMEM,
        scratch_shapes=[pltpu.VMEM((count, SLICE, LANES), jnp.bfloat16)],
        cost_estimate=pl.CostEstimate(
            flops=2 * count * Y * SLICE * SLICE * LANES * 2,
            bytes_accessed=count * Y * SLICE * SLICE * 2,
            transcendentals=0,
        ),
    )(meta, tiles, slots)


def summed_over_col(meta_send, meta_keep, tiles, slots):
    sent = apply_half(meta_send, tiles, slots)
    received = lax.ppermute(sent, "core", [(0, 1), (1, 0)])
    kept = apply_half(meta_keep, tiles, slots)
    pieces = lax.all_to_all(kept + received, "y", 0, 0)
    return jnp.sum(pieces, axis=0)


def total_over_all(value):
    value = value + lax.ppermute(value, "core", [(0, 1), (1, 0)])
    for axes, size in ((("x", "y"), X * Y), (("z",), Z)):
        copies = jnp.broadcast_to(value[None], (size,) + value.shape)
        value = jnp.sum(lax.all_to_all(copies, axes, 0, 0), axis=0)
    return value


def gram_kernel(spread, third, first, filtered, gram):
    value = 4.0 * third[...] - 3.0 * spread[0] * first[...]
    filtered[...] = value
    full = lax.dot_general(
        value, value, (((0,), (0,)), ((), ())), precision=HIGHEST, preferred_element_type=jnp.float32
    )
    half = LANES // 2
    gram64 = full[:half, :half] + full[half:, half:]
    gram[...] = jnp.concatenate([gram64[: half // 2], gram64[half // 2 :]], axis=1)


def finish_kernel(scale, gram, filtered, out):
    half = LANES // 2
    packed = gram[...]
    square = jnp.concatenate([packed[:, :half], packed[:, half:]], axis=0)
    row = lax.broadcasted_iota(jnp.int32, (half, LANES), 0)
    lane = lax.broadcasted_iota(jnp.int32, (half, LANES), 1)
    unit = jnp.where(lane - half == row, 1.0, 0.0)
    work = jnp.where(lane < half, jnp.concatenate([square, square], axis=1), unit)
    rows = lax.broadcasted_iota(jnp.int32, (half, 1), 0)
    pivots = jnp.zeros((half, 1), jnp.float32)
    for k in range(half):
        column = work[:, k : k + 1]
        pivot = work[k : k + 1, k : k + 1]
        pivots = jnp.where(rows == k, pivot, pivots)
        factor = jnp.where(rows > k, column / pivot, 0.0)
        work = work - factor * work[k : k + 1, :]
    inverse = work[:, half:] * (scale / jnp.sqrt(pivots))
    for block in range(2):
        out[block] = lax.dot_general(
            inverse,
            filtered[:, block * half : (block + 1) * half],
            (((1,), (1,)), ((), ())),
            precision=HIGHEST,
            preferred_element_type=jnp.float32,
        )


def on_device(tiles, tile_row, tile_col, tile_count, block_vectors):
    blocks, rows, vectors = block_vectors.shape
    count = tiles.shape[0]
    core = lax.axis_index("core")
    live = (jnp.arange(count, dtype=jnp.int32) < tile_count[0]).astype(jnp.int32)
    per_tile = jnp.stack([(tile_col // 2) % Z, tile_col % 2, tile_row, live], axis=1).reshape(-1)
    meta_keep = jnp.concatenate([core[None], per_tile])
    meta_send = jnp.concatenate([1 - core[None], per_tile])

    packed = block_vectors.transpose(1, 0, 2).reshape(rows, blocks * vectors)
    apply = functools.partial(summed_over_col, meta_send, meta_keep, tiles)
    first = apply(window(packed))
    second = apply(window(first.astype(jnp.bfloat16)))
    wide = packed.astype(jnp.float32)
    sums = jnp.stack([jnp.sum(first * first, axis=0), jnp.sum(wide * wide, axis=0)])
    sums = total_over_all(jnp.concatenate([sums, jnp.zeros((6, LANES), jnp.float32)]))
    spread = jnp.sum(sums[0]) / jnp.sum(sums[1])
    third = apply(window(second.astype(jnp.bfloat16)))

    filtered, gram = pl.pallas_call(
        gram_kernel,
        out_shape=(
            jax.ShapeDtypeStruct((rows, LANES), jnp.float32),
            jax.ShapeDtypeStruct((vectors // 2, LANES), jnp.float32),
        ),
        in_specs=[SMEM, VMEM, VMEM],
        out_specs=(VMEM, VMEM),
    )(spread[None], third, first)
    gram = total_over_all(gram)
    total_rows = blocks * rows * X * Z * Y * CORE
    out = pl.pallas_call(
        functools.partial(finish_kernel, math.sqrt(total_rows)),
        out_shape=jax.ShapeDtypeStruct((blocks, vectors, rows), jnp.float32),
        in_specs=[VMEM, VMEM],
        out_specs=VMEM,
    )(gram, filtered)
    return out.transpose(0, 2, 1)


def solution(mesh):
    grid = Mesh(mesh.devices.reshape(X, Z, Y, CORE), ALL)
    row, col = ("x", "z"), ("y", "core")
    in_specs = (P(row, None, col), P(row), P(row), P(row), P(row, col, None))
    return jax.shard_map(
        on_device, mesh=grid, in_specs=in_specs, out_specs=P(row, col, None), check_vma=False
    )
```

```python
import functools
import math

import jax
import jax.numpy as jnp
from jax import lax
from jax.experimental import pallas as pl
from jax.experimental.pallas import tpu as pltpu
from jax.sharding import Mesh, PartitionSpec as P

X, Z, Y, CORE = 4, 8, 4, 2
ALL = ("x", "z", "y", "core")
SLICE = 256
LANES = 128
HALF = LANES // 2
EXT = 16
SUMS = 8
HIGHEST = lax.Precision.HIGHEST
VMEM = pl.BlockSpec(memory_space=pltpu.VMEM)
SMEM = pl.BlockSpec(memory_space=pltpu.SMEM)
F32, BF16 = jnp.float32, jnp.bfloat16


def call(kernel, outs, specs, *args, scratch=(), limit=8, flops=0, moved=0):
    single = not isinstance(outs[0][0], tuple)
    shapes = (outs,) if single else outs
    result = pl.pallas_call(
        kernel,
        out_shape=tuple(jax.ShapeDtypeStruct(*s) for s in shapes),
        in_specs=specs,
        out_specs=(VMEM,) * len(shapes),
        scratch_shapes=scratch,
        compiler_params=pltpu.CompilerParams(vmem_limit_bytes=limit << 20),
        cost_estimate=pl.CostEstimate(flops=flops, bytes_accessed=moved, transcendentals=0),
    )(*args)
    return result[0] if single else result


def x_neighbour_pairs():
    pairs = []
    for x in range(X):
        for z in range(Z):
            to = (x + 1) % X if z >= Z // 2 else (x - 1) % X
            for c in range(Y * CORE):
                pairs.append(((x * Z + z) * Y * CORE + c, (to * Z + z) * Y * CORE + c))
    return pairs


def split(value):
    high = value.astype(BF16).astype(F32)
    rest = value - high
    middle = rest.astype(BF16).astype(F32)
    return jnp.concatenate([high, middle, rest - middle], axis=0)


def joined(rows):
    return rows[0:2] + rows[2:4] + rows[4:6]


def pad_rows(value, count):
    return jnp.concatenate([value, jnp.zeros((count - value.shape[0], LANES), F32)], axis=0)


def pieces_kernel(stage, meta, own, other, *refs):
    out = refs[-1]
    z = meta[1]
    half = Z // 2
    for target in range(Z):
        use_other = jnp.where(z < half, z <= target - half - 1, z >= target + half)

        @pl.when(use_other)
        def _():
            out[target, :SLICE] = other[:SLICE]

        @pl.when(jnp.logical_not(use_other))
        def _():
            out[target, :SLICE] = own[:SLICE]

    if stage == 0:
        return
    theirs = other[SLICE:].astype(F32)
    if stage == 1:
        mine = own[SLICE:].astype(F32)
        extra = pad_rows(jnp.concatenate([mine[:6], theirs[:6]], axis=0), EXT)
    else:
        extra = pad_rows(split(refs[0][0:2] + joined(theirs)), EXT)
    extra = extra.astype(BF16)
    for target in range(Z):
        out[target, SLICE:] = extra


def window(stage, meta, own, *parts):
    other = lax.ppermute(own, ALL, x_neighbour_pairs())
    specs = [SMEM] + [VMEM] * (2 + len(parts))
    shape = (Z,) + own.shape
    pieces = call(functools.partial(pieces_kernel, stage), (shape, BF16), specs, meta, own, other, *parts)
    return lax.all_to_all(pieces, "z", 0, 0)


def multiply(meta, first_slice, tiles, rhs, out, sums):
    count = tiles.shape[0]
    for y in range(Y):
        start = pl.multiple_of((y * CORE + first_slice) * SLICE, SLICE)
        total = jnp.zeros((SLICE, LANES), F32)
        for t in range(count):
            total = total + jnp.dot(
                tiles[t, pl.ds(start, SLICE), :], rhs[t], preferred_element_type=F32
            )
        out[y, :SLICE] = total
        if sums is not None:
            out[y, SLICE:] = sums


def send_kernel(stage, meta, tiles, slots, out, rhs, *sums_ref):
    lane = lax.broadcasted_iota(jnp.int32, (SLICE, LANES), 1)
    for t in range(tiles.shape[0]):
        slot, parity, block, live = (meta[2 + 4 * t + i] for i in range(4))
        vectors = slots[slot, :SLICE].astype(F32)
        turned = pltpu.roll(vectors, HALF, axis=1)
        vectors = jnp.where(parity == block, vectors, turned)
        first = block * HALF
        keep = (lane >= first) & (lane < first + HALF) & (live > 0)
        rhs[t] = jnp.where(keep, vectors, 0.0).astype(BF16)
    sums = None
    if stage:
        extra = [slots[z, SLICE:].astype(F32) for z in range(Z)]
    if stage == 1:
        low, high = sum(extra[: Z // 2]), sum(extra[Z // 2 :])
        own_low, own_high = joined(low), joined(high)
        next_low, next_high = joined(low[6:12]), joined(high[6:12])
        upper = meta[1] >= Z // 2
        gathered = jnp.where(upper, own_high + next_high, own_low + next_low)
        passed = jnp.where(upper, next_high + own_low, next_low + own_high)
        sums = pad_rows(jnp.concatenate([gathered, passed], axis=0), SUMS)
        sums_ref[0][...] = sums
    if stage == 2:
        sums_ref[0][...] = pad_rows(joined(extra[0]) + joined(extra[Z // 2]), SUMS)
    multiply(meta, 1 - meta[0], tiles, rhs, out, sums)


def keep_kernel(stage, meta, tiles, rhs, *refs):
    sums = refs[0][...] if stage == 1 else None
    multiply(meta, meta[0], tiles, rhs, refs[-1], sums)


def apply_graph(stage, meta, tiles, slots):
    count = tiles.shape[0]
    rows = SLICE + (SUMS if stage == 1 else 0)
    work = dict(limit=20, flops=2 * count * Y * SLICE * SLICE * LANES, moved=count * Y * SLICE * SLICE * 2)
    outs = (((Y, rows, LANES), F32), ((count, SLICE, LANES), BF16))
    if stage:
        outs += (((SUMS, LANES), F32),)
    sent, rhs, *sums = call(
        functools.partial(send_kernel, stage), outs, [SMEM, VMEM, VMEM], meta, tiles, slots, **work
    )
    received = lax.ppermute(sent, "core", [(0, 1), (1, 0)])
    passed = sums if stage == 1 else []
    kept = call(
        functools.partial(keep_kernel, stage),
        outs[0],
        [SMEM] + [VMEM] * (2 + len(passed)),
        meta,
        tiles,
        rhs,
        *passed,
        **work,
    )
    return lax.all_to_all(kept + received, "y", 0, 0), sums


def first_kernel(pieces, vectors, first, payload):
    value = pieces[0] + pieces[1] + pieces[2] + pieces[3]
    first[...] = value
    payload[:SLICE] = value.astype(BF16)
    wide = vectors[...].astype(F32)
    sums = [jnp.sum(part * part, axis=0, keepdims=True) for part in (value, wide)]
    payload[SLICE:] = pad_rows(split(jnp.concatenate(sums, axis=0)), EXT).astype(BF16)


def second_kernel(pieces, payload, gathered):
    value = pieces[0] + pieces[1] + pieces[2] + pieces[3]
    payload[:SLICE] = value[:SLICE].astype(BF16)
    sums = value[SLICE:]
    gathered[...] = sums
    payload[SLICE:] = pad_rows(split(sums[2:4]), EXT).astype(BF16)


def gram_kernel(pieces, first, sums, filtered, gram):
    third = pieces[0] + pieces[1] + pieces[2] + pieces[3]
    totals = jnp.sum(sums[...], axis=1, keepdims=True)
    spread = totals[0:1] / totals[1:2]
    value = 4.0 * third - 3.0 * spread * first[...]
    filtered[...] = value
    full = lax.dot_general(
        value, value, (((0,), (0,)), ((), ())), precision=HIGHEST, preferred_element_type=F32
    )
    gram64 = full[:HALF, :HALF] + full[HALF:, HALF:]
    gram[...] = jnp.concatenate([gram64[: HALF // 2], gram64[HALF // 2 :]], axis=1)


def finish_kernel(scale, grams, filtered, out):
    packed = grams[0]
    for i in range(1, grams.shape[0]):
        packed = packed + grams[i]
    square = jnp.concatenate([packed[:, :HALF], packed[:, HALF:]], axis=0)
    row = lax.broadcasted_iota(jnp.int32, (HALF, LANES), 0)
    lane = lax.broadcasted_iota(jnp.int32, (HALF, LANES), 1)
    unit = jnp.where(lane - HALF == row, 1.0, 0.0)
    work = jnp.where(lane < HALF, jnp.concatenate([square, square], axis=1), unit)
    rows = lax.broadcasted_iota(jnp.int32, (HALF, 1), 0)
    for k in range(HALF - 1):
        scaled = work[k : k + 1, :] * (1.0 / work[k : k + 1, k : k + 1])
        column = jnp.where(rows > k, work[:, k : k + 1], 0.0)
        work = work - column * scaled
    pivots = jnp.sum(jnp.where(lane == row, work, 0.0), axis=1, keepdims=True)
    inverse = work[:, HALF:] * (scale / jnp.sqrt(pivots))
    for block in range(2):
        out[block] = lax.dot_general(
            inverse,
            filtered[:, block * HALF : (block + 1) * HALF],
            (((1,), (1,)), ((), ())),
            precision=HIGHEST,
            preferred_element_type=F32,
        )


def on_device(tiles, tile_row, tile_col, tile_count, block_vectors):
    blocks, rows, vectors = block_vectors.shape
    count = tiles.shape[0]
    place = jnp.stack([lax.axis_index("core"), lax.axis_index("z")])
    live = (jnp.arange(count, dtype=jnp.int32) < tile_count[0]).astype(jnp.int32)
    per_tile = jnp.stack([(tile_col // 2) % Z, tile_col % 2, tile_row, live], axis=1)
    meta = jnp.concatenate([place, per_tile.reshape(-1)])

    packed = block_vectors.transpose(1, 0, 2).reshape(rows, blocks * vectors)
    slice_shape, payload_shape = (rows, LANES), (rows + EXT, LANES)

    pieces, _ = apply_graph(0, meta, tiles, window(0, meta, packed))
    first, payload = call(
        first_kernel, ((slice_shape, F32), (payload_shape, BF16)), [VMEM, VMEM], pieces, packed
    )
    pieces, _ = apply_graph(1, meta, tiles, window(1, meta, payload))
    payload, gathered = call(
        second_kernel, ((payload_shape, BF16), ((SUMS, LANES), F32)), [VMEM], pieces
    )
    pieces, sums = apply_graph(2, meta, tiles, window(2, meta, payload, gathered))
    filtered, gram = call(
        gram_kernel,
        ((slice_shape, F32), ((vectors // 2, LANES), F32)),
        [VMEM] * 3,
        pieces,
        first,
        *sums,
    )

    gram = gram + lax.ppermute(gram, "core", [(0, 1), (1, 0)])
    grams = lax.all_to_all(jnp.broadcast_to(gram[None], (X * Y,) + gram.shape), ("x", "y"), 0, 0)
    gram = jnp.sum(grams, axis=0)
    grams = lax.all_to_all(jnp.broadcast_to(gram[None], (Z,) + gram.shape), "z", 0, 0)
    total_rows = blocks * rows * X * Z * Y * CORE
    out = call(
        functools.partial(finish_kernel, math.sqrt(total_rows)),
        ((blocks, vectors, rows), F32),
        [VMEM, VMEM],
        grams,
        filtered,
    )
    return out.transpose(0, 2, 1)


def solution(mesh):
    grid = Mesh(mesh.devices.reshape(X, Z, Y, CORE), ALL)
    row, col = ("x", "z"), ("y", "core")
    in_specs = (P(row, None, col), P(row), P(row), P(row), P(row, col, None))
    return jax.shard_map(
        on_device, mesh=grid, in_specs=in_specs, out_specs=P(row, col, None), check_vma=False
    )
```

```python
import functools
import math

import jax
import jax.numpy as jnp
from jax import lax
from jax.experimental import pallas as pl
from jax.experimental.pallas import tpu as pltpu
from jax.sharding import Mesh, PartitionSpec as P

X, Z, Y, CORE = 4, 8, 4, 2
ALL = ("x", "z", "y", "core")
SLICE = 256
LANES = 128
HALF = LANES // 2
EXT = 16
SUMS = 8
HIGHEST = lax.Precision.HIGHEST
VMEM = pl.BlockSpec(memory_space=pltpu.VMEM)
SMEM = pl.BlockSpec(memory_space=pltpu.SMEM)
F32, BF16 = jnp.float32, jnp.bfloat16


def call(kernel, outs, specs, *args, scratch=(), limit=8, flops=0, moved=0):
    single = not isinstance(outs[0][0], tuple)
    shapes = (outs,) if single else outs
    result = pl.pallas_call(
        kernel,
        out_shape=tuple(jax.ShapeDtypeStruct(*s) for s in shapes),
        in_specs=specs,
        out_specs=(VMEM,) * len(shapes),
        scratch_shapes=scratch,
        compiler_params=pltpu.CompilerParams(vmem_limit_bytes=limit << 20),
        cost_estimate=pl.CostEstimate(flops=flops, bytes_accessed=moved, transcendentals=0),
    )(*args)
    return result[0] if single else result


def x_neighbour_pairs():
    pairs = []
    for x in range(X):
        for z in range(Z):
            to = (x + 1) % X if z >= Z // 2 else (x - 1) % X
            for c in range(Y * CORE):
                pairs.append(((x * Z + z) * Y * CORE + c, (to * Z + z) * Y * CORE + c))
    return pairs


def split(value):
    high = value.astype(BF16).astype(F32)
    rest = value - high
    middle = rest.astype(BF16).astype(F32)
    return jnp.concatenate([high, middle, rest - middle], axis=0)


def joined(rows):
    return rows[0:2] + rows[2:4] + rows[4:6]


def pad_rows(value, count):
    return jnp.concatenate([value, jnp.zeros((count - value.shape[0], LANES), F32)], axis=0)


def place_kernel(tiles, token):
    token[...] = jnp.zeros_like(token)


def turned(value):
    return value.astype(F32).T.astype(BF16)


def pieces_kernel(stage, own, other, *refs):
    out = refs[-1]
    z = lax.axis_index("z")
    half = Z // 2
    if stage == 0:
        mine, theirs = turned(own[...]), turned(other[...])
    else:
        mine, theirs = own[:SLICE], other[:SLICE]
    for target in range(Z):
        use_other = jnp.where(z < half, z <= target - half - 1, z >= target + half)

        @pl.when(use_other)
        def _():
            out[target, :SLICE] = theirs

        @pl.when(jnp.logical_not(use_other))
        def _():
            out[target, :SLICE] = mine

    if stage == 0:
        return
    theirs = other[SLICE:].astype(F32)
    if stage == 1:
        mine = own[SLICE:].astype(F32)
        extra = pad_rows(jnp.concatenate([mine[:6], theirs[:6]], axis=0), EXT)
    else:
        extra = pad_rows(split(refs[0][0:2] + joined(theirs)), EXT)
    extra = extra.astype(BF16)
    for target in range(Z):
        out[target, SLICE:] = extra


def window(stage, own, *parts):
    other = lax.ppermute(own, ALL, x_neighbour_pairs())
    rows = SLICE if stage == 0 else SLICE + EXT
    pieces = call(
        functools.partial(pieces_kernel, stage),
        ((Z, rows, LANES), BF16),
        [VMEM] * (2 + len(parts)),
        own,
        other,
        *parts,
    )
    return lax.all_to_all(pieces, "z", 0, 0)


def multiply(core, steps, tiles, rhs, out, sums):
    y = lax.axis_index("y")
    for i, step in enumerate(steps):
        start = pl.multiple_of((lax.rem(y + step, Y) * CORE + core) * SLICE, SLICE)
        total = jnp.zeros((SLICE, LANES), F32)
        for t in range(tiles.shape[0]):
            total = total + jnp.dot(
                tiles[t, pl.ds(start, SLICE), :], rhs[t], preferred_element_type=F32
            )
        out[i, :SLICE] = total
        if sums is not None:
            out[i, SLICE:] = sums


def send_kernel(stage, tile_row, tile_col, tile_count, tiles, slots, out, rhs, *sums_ref):
    lane = lax.broadcasted_iota(jnp.int32, (SLICE, LANES), 1)
    for t in range(tiles.shape[0]):
        slot = lax.rem(lax.div(tile_col[t], 2), Z)
        first = tile_row[t] * HALF
        vectors = slots[slot, :SLICE].astype(F32)
        other_half = pltpu.roll(vectors, HALF, axis=1)
        vectors = jnp.where(lax.rem(tile_col[t], 2) == tile_row[t], vectors, other_half)
        keep = (lane >= first) & (lane < first + HALF) & (t < tile_count[0])
        rhs[t] = jnp.where(keep, vectors, 0.0).astype(BF16)
    sums = None
    if stage:
        extra = [slots[z, SLICE:].astype(F32) for z in range(Z)]
    if stage == 1:
        low, high = sum(extra[: Z // 2]), sum(extra[Z // 2 :])
        own_low, own_high = joined(low), joined(high)
        next_low, next_high = joined(low[6:12]), joined(high[6:12])
        upper = lax.axis_index("z") >= Z // 2
        gathered = jnp.where(upper, own_high + next_high, own_low + next_low)
        passed = jnp.where(upper, next_high + own_low, next_low + own_high)
        sums = pad_rows(jnp.concatenate([gathered, passed], axis=0), SUMS)
        sums_ref[0][...] = sums
    if stage == 2:
        sums_ref[0][...] = pad_rows(joined(extra[0]) + joined(extra[Z // 2]), SUMS)
    multiply(1 - lax.axis_index("core"), range(Y), tiles, rhs, out, sums)


def keep_kernel(stage, steps, tiles, rhs, *refs):
    sums = refs[0][...] if stage == 1 else None
    multiply(lax.axis_index("core"), steps, tiles, rhs, refs[-1], sums)


def apply_graph(stage, plan, tiles, slots):
    count = tiles.shape[0]
    rows = SLICE + (SUMS if stage == 1 else 0)

    def work(slices):
        return dict(
            limit=20,
            flops=2 * count * slices * SLICE * SLICE * LANES,
            moved=count * slices * SLICE * SLICE * 2,
        )

    outs = (((Y, rows, LANES), F32), ((count, SLICE, LANES), BF16))
    if stage:
        outs += (((SUMS, LANES), F32),)
    sent, rhs, *sums = call(
        functools.partial(send_kernel, stage), outs, [SMEM] * 3 + [VMEM] * 2, *plan, tiles, slots, **work(Y)
    )
    received = lax.ppermute(sent, "core", [(0, 1), (1, 0)])
    passed = sums if stage == 1 else []

    def keep(steps):
        return call(
            functools.partial(keep_kernel, stage, steps),
            ((len(steps), rows, LANES), F32),
            [VMEM] * (2 + len(passed)),
            tiles,
            rhs,
            *passed,
            **work(len(steps)),
        )

    away = keep(range(1, Y))
    parts = []
    for step in (2, 1, 3):
        part = away[step - 1] + received[step]
        parts.append(lax.ppermute(part, "y", [(y, (y + step) % Y) for y in range(Y)]))
    return (keep((0,)), received, *parts), sums


def added(refs):
    own, received, *parts = refs
    value = own[0] + received[0]
    for part in parts:
        value = value + part[...]
    return value


def first_kernel(*refs):
    vectors, first, payload = refs[-3:]
    value = added(refs[:-3])
    first[...] = value
    payload[:SLICE] = value.astype(BF16)
    wide = vectors[...].astype(F32)
    wide = jnp.sum(wide * wide, axis=0, keepdims=True)
    sums = jnp.sum(value * value, axis=0, keepdims=True)
    sums = jnp.concatenate([sums, wide[:, :LANES] + wide[:, LANES:]], axis=0)
    payload[SLICE:] = pad_rows(split(sums), EXT).astype(BF16)


def second_kernel(*refs):
    payload, gathered = refs[-2:]
    value = added(refs[:-2])
    payload[:SLICE] = value[:SLICE].astype(BF16)
    sums = value[SLICE:]
    gathered[...] = sums
    payload[SLICE:] = pad_rows(split(sums[2:4]), EXT).astype(BF16)


def gram_kernel(*refs):
    first, sums, filtered, gram = refs[-4:]
    third = added(refs[:-4])
    totals = jnp.sum(sums[...], axis=1, keepdims=True)
    spread = totals[0:1] / totals[1:2]
    value = 4.0 * third - 3.0 * spread * first[...]
    filtered[...] = value
    full = lax.dot_general(
        value, value, (((0,), (0,)), ((), ())), precision=HIGHEST, preferred_element_type=F32
    )
    gram64 = full[:HALF, :HALF] + full[HALF:, HALF:]
    gram[...] = jnp.concatenate([gram64[: HALF // 2], gram64[HALF // 2 :]], axis=1)


def inverse_factor(work):
    step = 8
    shape = (step, LANES)
    groups = [work[i : i + step] for i in range(0, HALF, step)]
    row = lax.broadcasted_iota(jnp.int32, shape, 0)
    for g in range(len(groups)):
        rest = range(g, len(groups))
        columns = [
            {h: jnp.broadcast_to(groups[h][:, step * g + j : step * g + j + 1], shape) for h in rest}
            for j in range(step)
        ]
        entries = [
            [jnp.broadcast_to(columns[j][g][i : i + 1], shape) for j in range(i + 1)] for i in range(step)
        ]
        rows = [jnp.broadcast_to(groups[g][i : i + 1], shape) for i in range(step)]
        pivots = entries[0][0]
        for j in range(step):
            pivot = entries[j][j]
            pivots = jnp.where(row == j, pivot, pivots)
            reciprocal = 1.0 / pivot
            scaled = rows[j] * reciprocal
            for i in range(j + 1, step):
                factor = entries[i][j] * reciprocal
                rows[i] = rows[i] - factor * rows[j]
                for m in range(j + 1, i + 1):
                    entries[i][m] = entries[i][m] - factor * entries[m][j]
                for h in rest:
                    columns[i][h] = columns[i][h] - factor * columns[j][h]
            for h in rest:
                column = columns[j][h]
                if h == g:
                    column = jnp.where(row > j, column, 0.0)
                groups[h] = groups[h] - column * scaled
        groups[g] = groups[g] / jnp.sqrt(pivots)
    return jnp.concatenate(groups, axis=0)


def finish_kernel(scale, grams, filtered, out):
    packed = grams[0]
    for i in range(1, grams.shape[0]):
        packed = packed + grams[i]
    square = jnp.concatenate([packed[:, :HALF], packed[:, HALF:]], axis=0)
    row = lax.broadcasted_iota(jnp.int32, (HALF, LANES), 0)
    lane = lax.broadcasted_iota(jnp.int32, (HALF, LANES), 1)
    unit = jnp.where(lane - HALF == row, 1.0, 0.0)
    work = jnp.where(lane < HALF, jnp.concatenate([square, square], axis=1), unit)
    inverse = inverse_factor(work)[:, HALF:] * scale
    for block in range(2):
        out[block] = lax.dot_general(
            inverse,
            filtered[:, block * HALF : (block + 1) * HALF],
            (((1,), (1,)), ((), ())),
            precision=HIGHEST,
            preferred_element_type=F32,
        )


def on_device(tiles, tile_row, tile_col, tile_count, block_vectors):
    blocks, rows, vectors = block_vectors.shape
    count = tiles.shape[0]
    plan = (tile_row, tile_col, tile_count)
    vectors_turned = block_vectors.transpose(0, 2, 1).reshape(blocks * vectors, rows)
    slice_shape, payload_shape = (rows, LANES), (rows + EXT, LANES)
    token = call(place_kernel, ((SUMS, LANES), F32), [VMEM], tiles, limit=20, moved=2 * tiles.size)
    parts, _ = apply_graph(0, plan, tiles, window(0, vectors_turned, token))
    first, payload = call(
        first_kernel,
        ((slice_shape, F32), (payload_shape, BF16)),
        [VMEM] * (len(parts) + 1),
        *parts,
        vectors_turned,
    )
    parts, _ = apply_graph(1, plan, tiles, window(1, payload))
    payload, gathered = call(
        second_kernel,
        ((payload_shape, BF16), ((SUMS, LANES), F32)),
        [VMEM] * len(parts),
        *parts,
    )
    parts, sums = apply_graph(2, plan, tiles, window(2, payload, gathered))
    filtered, gram = call(
        gram_kernel,
        ((slice_shape, F32), ((vectors // 2, LANES), F32)),
        [VMEM] * (len(parts) + 2),
        *parts,
        first,
        *sums,
    )

    gram = gram + lax.ppermute(gram, "core", [(0, 1), (1, 0)])
    grams = lax.all_to_all(jnp.broadcast_to(gram[None], (X * Y,) + gram.shape), ("x", "y"), 0, 0)
    gram = jnp.sum(grams, axis=0)
    grams = lax.all_to_all(jnp.broadcast_to(gram[None], (Z,) + gram.shape), "z", 0, 0)
    total_rows = blocks * rows * X * Z * Y * CORE
    out = call(
        functools.partial(finish_kernel, math.sqrt(total_rows)),
        ((blocks, vectors, rows), F32),
        [VMEM, VMEM],
        grams,
        filtered,
    )
    return out.transpose(0, 2, 1)


def solution(mesh):
    grid = Mesh(mesh.devices.reshape(X, Z, Y, CORE), ALL)
    row, col = ("x", "z"), ("y", "core")
    in_specs = (P(row, None, col), P(row), P(row), P(row), P(row, col, None))
    return jax.shard_map(
        on_device, mesh=grid, in_specs=in_specs, out_specs=P(row, col, None), check_vma=False
    )
```

```python
import functools
import math

import jax
import jax.numpy as jnp
from jax import lax
from jax.experimental import pallas as pl
from jax.experimental.pallas import tpu as pltpu
from jax.sharding import Mesh, PartitionSpec as P

X, Z, Y, CORE = 4, 8, 4, 2
ALL = ("x", "z", "y", "core")
SLICE = 256
LANES = 128
HALF = LANES // 2
EXT = 16
SUMS = 8
CORE_SWAP = [(0, 1), (1, 0)]
HIGHEST = lax.Precision.HIGHEST
VMEM = pl.BlockSpec(memory_space=pltpu.VMEM)
SMEM = pl.BlockSpec(memory_space=pltpu.SMEM)
F32, BF16 = jnp.float32, jnp.bfloat16


def call(kernel, outs, specs, *args, scratch=(), limit=8, flops=0, moved=0):
    single = not isinstance(outs[0][0], tuple)
    shapes = (outs,) if single else outs
    result = pl.pallas_call(
        kernel,
        out_shape=tuple(jax.ShapeDtypeStruct(*s) for s in shapes),
        in_specs=specs,
        out_specs=(VMEM,) * len(shapes),
        scratch_shapes=scratch,
        compiler_params=pltpu.CompilerParams(vmem_limit_bytes=limit << 20),
        cost_estimate=pl.CostEstimate(flops=flops, bytes_accessed=moved, transcendentals=0),
    )(*args)
    return result[0] if single else result


def x_neighbour_pairs():
    pairs = []
    for x in range(X):
        for z in range(Z):
            to = (x + 1) % X if z >= Z // 2 else (x - 1) % X
            for c in range(Y * CORE):
                pairs.append(((x * Z + z) * Y * CORE + c, (to * Z + z) * Y * CORE + c))
    return pairs


def split(value):
    high = value.astype(BF16).astype(F32)
    rest = value - high
    middle = rest.astype(BF16).astype(F32)
    return jnp.concatenate([high, middle, rest - middle], axis=0)


def joined(rows):
    return rows[0:2] + rows[2:4] + rows[4:6]


def pad_rows(value, count):
    return jnp.concatenate([value, jnp.zeros((count - value.shape[0], LANES), F32)], axis=0)


def place_kernel(tiles, token):
    token[...] = jnp.zeros_like(token)


def turn_kernel(vectors, out):
    out[...] = vectors[...].astype(F32).T.astype(BF16)


def pieces_kernel(stage, own, other, *refs):
    out = refs[-1]
    z = lax.axis_index("z")
    half = Z // 2
    mine, theirs = own[:SLICE], other[:SLICE]
    for target in range(Z):
        use_other = jnp.where(z < half, z <= target - half - 1, z >= target + half)

        @pl.when(use_other)
        def _():
            out[target, :SLICE] = theirs

        @pl.when(jnp.logical_not(use_other))
        def _():
            out[target, :SLICE] = mine

    if stage == 0:
        return
    theirs = other[SLICE:].astype(F32)
    if stage == 1:
        mine = own[SLICE:].astype(F32)
        extra = pad_rows(jnp.concatenate([mine[:6], theirs[:6]], axis=0), EXT)
    else:
        extra = pad_rows(split(refs[0][0:2] + joined(theirs)), EXT)
    extra = extra.astype(BF16)
    for target in range(Z):
        out[target, SLICE:] = extra


def window(stage, own, *parts):
    other = lax.ppermute(own, ALL, x_neighbour_pairs())
    rows = SLICE if stage == 0 else SLICE + EXT
    pieces = call(
        functools.partial(pieces_kernel, stage),
        ((Z, rows, LANES), BF16),
        [VMEM] * (2 + len(parts)),
        own,
        other,
        *parts,
    )
    return lax.all_to_all(pieces, "z", 0, 0)


def multiply(core, tiles, rhs, out, sums):
    y = lax.axis_index("y")
    for i in range(Y):
        start = pl.multiple_of((lax.rem(y + i, Y) * CORE + core) * SLICE, SLICE)
        total = jnp.zeros((SLICE, LANES), F32)
        for t in range(tiles.shape[0]):
            total = total + jnp.dot(
                tiles[t, pl.ds(start, SLICE), :], rhs[t], preferred_element_type=F32
            )
        out[i, :SLICE] = total
        if sums is not None:
            out[i, SLICE:] = sums


def send_kernel(stage, tile_row, tile_col, tile_count, tiles, slots, out, rhs, *sums_ref):
    lane = lax.broadcasted_iota(jnp.int32, (SLICE, LANES), 1)
    for t in range(tiles.shape[0]):
        row, col = tile_row[t], tile_col[t]
        parity, slot = col & 1, lax.shift_right_logical(col, 1) & (Z - 1)
        live = t < tile_count[0]
        first = row * HALF
        vectors = slots[slot, :SLICE].astype(F32)
        other_half = pltpu.roll(vectors, HALF, axis=1)
        vectors = jnp.where(parity == row, vectors, other_half)
        keep = (lane >= first) & (lane < first + HALF) & live
        rhs[t] = jnp.where(keep, vectors, 0.0).astype(BF16)
    sums = None
    if stage:
        extra = [slots[z, SLICE:].astype(F32) for z in range(Z)]
    if stage == 1:
        low, high = sum(extra[: Z // 2]), sum(extra[Z // 2 :])
        own_low, own_high = joined(low), joined(high)
        next_low, next_high = joined(low[6:12]), joined(high[6:12])
        upper = lax.axis_index("z") >= Z // 2
        gathered = jnp.where(upper, own_high + next_high, own_low + next_low)
        passed = jnp.where(upper, next_high + own_low, next_low + own_high)
        sums = pad_rows(jnp.concatenate([gathered, passed], axis=0), SUMS)
        sums_ref[0][...] = sums
    if stage == 2:
        sums_ref[0][...] = pad_rows(joined(extra[0]) + joined(extra[Z // 2]), SUMS)
    multiply(1 - lax.axis_index("core"), tiles, rhs, out, sums)


def keep_kernel(stage, tiles, rhs, *refs):
    sums = refs[0][...] if stage == 1 else None
    multiply(lax.axis_index("core"), tiles, rhs, refs[-1], sums)


def apply_graph(stage, plan, tiles, slots):
    count = tiles.shape[0]
    rows = SLICE + (SUMS if stage == 1 else 0)
    slices = ((Y, rows, LANES), F32)
    outs = (slices, ((count, SLICE, LANES), BF16))
    if stage:
        outs += (((SUMS, LANES), F32),)
    size = dict(
        limit=20,
        flops=2 * count * Y * SLICE * SLICE * LANES,
        moved=count * Y * SLICE * SLICE * 2,
    )
    sent, rhs, *sums = call(
        functools.partial(send_kernel, stage),
        outs,
        [VMEM] * 5,
        *plan,
        tiles,
        slots,
        **size,
    )
    received = lax.ppermute(sent, "core", CORE_SWAP)
    given = [tiles, rhs] + (sums if stage == 1 else [])
    kept = call(functools.partial(keep_kernel, stage), slices, [VMEM] * len(given), *given, **size)
    parts = []
    for step in (3, 1, 2):
        part = kept[step] + received[step]
        parts.append(lax.ppermute(part, "y", [(y, (y + step) % Y) for y in range(Y)]))
    return (kept, received, *parts), sums


def added(refs):
    own, received, *parts = refs
    value = own[0] + received[0]
    for part in parts:
        value = value + part[...]
    return value


def first_kernel(*refs):
    vectors, first, payload = refs[-3:]
    value = added(refs[:-3])
    first[...] = value
    payload[:SLICE] = value.astype(BF16)
    wide = vectors[...].astype(F32)
    wide = jnp.sum(wide * wide, axis=0, keepdims=True)
    sums = jnp.concatenate([jnp.sum(value * value, axis=0, keepdims=True), wide], axis=0)
    payload[SLICE:] = pad_rows(split(sums), EXT).astype(BF16)


def second_kernel(*refs):
    payload, gathered = refs[-2:]
    value = added(refs[:-2])
    payload[:SLICE] = value[:SLICE].astype(BF16)
    sums = value[SLICE:]
    gathered[...] = sums
    payload[SLICE:] = pad_rows(split(sums[2:4]), EXT).astype(BF16)


def gram_kernel(*refs):
    first, sums, filtered, gram = refs[-4:]
    third = added(refs[:-4])
    totals = jnp.sum(sums[...], axis=1, keepdims=True)
    spread = totals[0:1] / totals[1:2]
    value = 4.0 * third - 3.0 * spread * first[...]
    filtered[...] = value
    full = lax.dot_general(
        value, value, (((0,), (0,)), ((), ())), precision=HIGHEST, preferred_element_type=F32
    )
    gram64 = full[:HALF, :HALF] + full[HALF:, HALF:]
    half = HALF // 2
    blocks = (gram64[:half, :half], gram64[half:, :half], gram64[half:, half:])
    gram[...] = jnp.concatenate(
        [
            jnp.concatenate([block[i : i + 8] for i in range(0, half, 8)], axis=1)
            for block in blocks
        ],
        axis=0,
    )


def inverse_factor(work):
    step = 8
    shape = (step, LANES)
    groups = [work[i : i + step] for i in range(0, HALF, step)]
    row = lax.broadcasted_iota(jnp.int32, shape, 0)
    for g in range(len(groups)):
        rest = range(g, len(groups))
        columns = [
            {h: jnp.broadcast_to(groups[h][:, step * g + j : step * g + j + 1], shape) for h in rest}
            for j in range(step)
        ]
        entries = [
            [jnp.broadcast_to(columns[j][g][i : i + 1], shape) for j in range(i + 1)] for i in range(step)
        ]
        rows = [jnp.broadcast_to(groups[g][i : i + 1], shape) for i in range(step)]
        pivots = entries[0][0]
        for j in range(step):
            pivot = entries[j][j]
            pivots = jnp.where(row == j, pivot, pivots)
            reciprocal = 1.0 / pivot
            scaled = rows[j] * reciprocal
            for i in range(j + 1, step):
                factor = entries[i][j] * reciprocal
                rows[i] = rows[i] - factor * rows[j]
                for m in range(j + 1, i + 1):
                    entries[i][m] = entries[i][m] - factor * entries[m][j]
                for h in rest:
                    columns[i][h] = columns[i][h] - factor * columns[j][h]
            for h in rest:
                column = columns[j][h]
                if h == g:
                    column = jnp.where(row > j, column, 0.0)
                groups[h] = groups[h] - column * scaled
        groups[g] = groups[g] / jnp.sqrt(pivots)
    return jnp.concatenate(groups, axis=0)


def finish_kernel(scale, grams, filtered, out):
    packed = grams[0]
    for i in range(1, grams.shape[0]):
        packed = packed + grams[i]
    half = HALF // 2
    top, corner, bottom = (
        jnp.concatenate([packed[b : b + 8, i : i + half] for i in range(0, LANES, half)], axis=0)
        for b in (0, 8, 16)
    )
    square = jnp.concatenate(
        [jnp.concatenate([top, corner.T], axis=1), jnp.concatenate([corner, bottom], axis=1)], axis=0
    )
    row = lax.broadcasted_iota(jnp.int32, (HALF, LANES), 0)
    lane = lax.broadcasted_iota(jnp.int32, (HALF, LANES), 1)
    unit = jnp.where(lane - HALF == row, 1.0, 0.0)
    work = jnp.where(lane < HALF, jnp.concatenate([square, square], axis=1), unit)
    inverse = inverse_factor(work)[:, HALF:] * scale
    for block in range(2):
        out[block] = lax.dot_general(
            inverse,
            filtered[:, block * HALF : (block + 1) * HALF],
            (((1,), (1,)), ((), ())),
            precision=HIGHEST,
            preferred_element_type=F32,
        )


def on_device(tiles, tile_row, tile_col, tile_count, block_vectors):
    blocks, rows, vectors = block_vectors.shape
    count = tiles.shape[0]
    plan = (tile_row, tile_col, tile_count)
    slice_shape, payload_shape = (rows, LANES), (rows + EXT, LANES)
    packed = block_vectors.transpose(0, 2, 1).reshape(blocks * vectors, rows)
    packed = call(turn_kernel, (slice_shape, BF16), [VMEM], packed)
    token = call(place_kernel, ((SUMS, LANES), F32), [VMEM], tiles, limit=20, moved=2 * tiles.size)
    parts, _ = apply_graph(0, plan, tiles, window(0, packed, *plan, token))
    first, payload = call(
        first_kernel,
        ((slice_shape, F32), (payload_shape, BF16)),
        [VMEM] * (len(parts) + 1),
        *parts,
        packed,
    )
    parts, _ = apply_graph(1, plan, tiles, window(1, payload))
    payload, gathered = call(
        second_kernel,
        ((payload_shape, BF16), ((SUMS, LANES), F32)),
        [VMEM] * len(parts),
        *parts,
    )
    parts, sums = apply_graph(2, plan, tiles, window(2, payload, gathered))
    filtered, gram = call(
        gram_kernel,
        ((slice_shape, F32), ((24, LANES), F32)),
        [VMEM] * (len(parts) + 2),
        *parts,
        first,
        *sums,
    )

    gram = gram + lax.ppermute(gram, "core", CORE_SWAP)
    grams = lax.all_to_all(jnp.broadcast_to(gram[None], (X * Y,) + gram.shape), ("x", "y"), 0, 0)
    gram = jnp.sum(grams, axis=0)
    grams = lax.all_to_all(jnp.broadcast_to(gram[None], (Z,) + gram.shape), "z", 0, 0)
    total_rows = blocks * rows * X * Z * Y * CORE
    out = call(
        functools.partial(finish_kernel, math.sqrt(total_rows)),
        ((blocks, vectors, rows), F32),
        [VMEM] * 2,
        grams,
        filtered,
    )
    return out.transpose(0, 2, 1)


def solution(mesh):
    grid = Mesh(mesh.devices.reshape(X, Z, Y, CORE), ALL)
    row, col = ("x", "z"), ("y", "core")
    in_specs = (P(row, None, col), P(row), P(row), P(row), P(row, col, None))
    return jax.shard_map(
        on_device, mesh=grid, in_specs=in_specs, out_specs=P(row, col, None), check_vma=False
    )
```

```python
import functools
import math

import jax
import jax.numpy as jnp
from jax import lax
from jax.experimental import pallas as pl
from jax.experimental.pallas import tpu as pltpu
from jax.sharding import Mesh, PartitionSpec as P

X, Z, Y, CORE = 4, 8, 4, 2
ALL = ("x", "z", "y", "core")
SLICE = 256
LANES = 128
HALF = LANES // 2
EXT = 16
SUMS = 8
CORE_SWAP = [(0, 1), (1, 0)]
HIGHEST = lax.Precision.HIGHEST
VMEM = pl.BlockSpec(memory_space=pltpu.VMEM)
SMEM = pl.BlockSpec(memory_space=pltpu.SMEM)
F32, BF16 = jnp.float32, jnp.bfloat16


def call(kernel, outs, specs, *args, scratch=(), limit=8, flops=0, moved=0):
    single = not isinstance(outs[0][0], tuple)
    shapes = (outs,) if single else outs
    result = pl.pallas_call(
        kernel,
        out_shape=tuple(jax.ShapeDtypeStruct(*s) for s in shapes),
        in_specs=specs,
        out_specs=(VMEM,) * len(shapes),
        scratch_shapes=scratch,
        compiler_params=pltpu.CompilerParams(vmem_limit_bytes=limit << 20),
        cost_estimate=pl.CostEstimate(flops=flops, bytes_accessed=moved, transcendentals=0),
    )(*args)
    return result[0] if single else result


def x_neighbour_pairs():
    pairs = []
    for x in range(X):
        for z in range(Z):
            to = (x + 1) % X if z >= Z // 2 else (x - 1) % X
            for c in range(Y * CORE):
                pairs.append(((x * Z + z) * Y * CORE + c, (to * Z + z) * Y * CORE + c))
    return pairs


def split(value):
    high = value.astype(BF16).astype(F32)
    rest = value - high
    middle = rest.astype(BF16).astype(F32)
    return jnp.concatenate([high, middle, rest - middle], axis=0)


def joined(rows):
    return rows[0:2] + rows[2:4] + rows[4:6]


def pad_rows(value, count):
    return jnp.concatenate([value, jnp.zeros((count - value.shape[0], LANES), F32)], axis=0)


def place_kernel(tiles, token):
    token[...] = jnp.zeros_like(token)


def turn_kernel(vectors, out):
    out[...] = vectors[...].astype(F32).T.astype(BF16)


def pieces_kernel(stage, own, other, *refs):
    out = refs[-1]
    z = lax.axis_index("z")
    half = Z // 2
    mine, theirs = own[:SLICE], other[:SLICE]
    for target in range(Z):
        use_other = jnp.where(z < half, z <= target - half - 1, z >= target + half)

        @pl.when(use_other)
        def _():
            out[target, :SLICE] = theirs

        @pl.when(jnp.logical_not(use_other))
        def _():
            out[target, :SLICE] = mine

    if stage == 0:
        return
    theirs = other[SLICE:].astype(F32)
    if stage == 1:
        mine = own[SLICE:].astype(F32)
        extra = pad_rows(jnp.concatenate([mine[:6], theirs[:6]], axis=0), EXT)
    else:
        extra = pad_rows(split(refs[0][0:2] + joined(theirs)), EXT)
    extra = extra.astype(BF16)
    for target in range(Z):
        out[target, SLICE:] = extra


def window(stage, own, *parts):
    other = lax.ppermute(own, ALL, x_neighbour_pairs())
    rows = SLICE if stage == 0 else SLICE + EXT
    pieces = call(
        functools.partial(pieces_kernel, stage),
        ((Z, rows, LANES), BF16),
        [VMEM] * (2 + len(parts)),
        own,
        other,
        *parts,
    )
    return lax.all_to_all(pieces, "z", 0, 0)


def multiply(core, tiles, rhs, out, sums):
    y = lax.axis_index("y")
    for i in range(Y):
        start = pl.multiple_of((lax.rem(y + i, Y) * CORE + core) * SLICE, SLICE)
        total = jnp.zeros((SLICE, LANES), F32)
        for t in range(tiles.shape[0]):
            total = total + jnp.dot(
                tiles[t, pl.ds(start, SLICE), :], rhs[t], preferred_element_type=F32
            )
        out[i, :SLICE] = total
        if sums is not None:
            out[i, SLICE:] = sums


def send_kernel(stage, tile_row, tile_col, tile_count, tiles, slots, out, rhs, *sums_ref):
    lane = lax.broadcasted_iota(jnp.int32, (SLICE, LANES), 1)
    for t in range(tiles.shape[0]):
        row, col = tile_row[t], tile_col[t]
        parity, slot = col & 1, lax.shift_right_logical(col, 1) & (Z - 1)
        live = t < tile_count[0]
        first = row * HALF
        vectors = slots[slot, :SLICE].astype(F32)
        other_half = pltpu.roll(vectors, HALF, axis=1)
        vectors = jnp.where(parity == row, vectors, other_half)
        keep = (lane >= first) & (lane < first + HALF) & live
        rhs[t] = jnp.where(keep, vectors, 0.0).astype(BF16)
    sums = None
    if stage:
        extra = [slots[z, SLICE:].astype(F32) for z in range(Z)]
    if stage == 1:
        low, high = sum(extra[: Z // 2]), sum(extra[Z // 2 :])
        own_low, own_high = joined(low), joined(high)
        next_low, next_high = joined(low[6:12]), joined(high[6:12])
        upper = lax.axis_index("z") >= Z // 2
        gathered = jnp.where(upper, own_high + next_high, own_low + next_low)
        passed = jnp.where(upper, next_high + own_low, next_low + own_high)
        sums = pad_rows(jnp.concatenate([gathered, passed], axis=0), SUMS)
        sums_ref[0][...] = sums
    if stage == 2:
        sums_ref[0][...] = pad_rows(joined(extra[0]) + joined(extra[Z // 2]), SUMS)
    multiply(1 - lax.axis_index("core"), tiles, rhs, out, sums)


def keep_kernel(stage, tiles, rhs, *refs):
    sums = refs[0][...] if stage == 1 else None
    multiply(lax.axis_index("core"), tiles, rhs, refs[-1], sums)


def apply_graph(stage, plan, tiles, slots):
    count = tiles.shape[0]
    rows = SLICE + (SUMS if stage == 1 else 0)
    slices = ((Y, rows, LANES), F32)
    outs = (slices, ((count, SLICE, LANES), BF16))
    if stage:
        outs += (((SUMS, LANES), F32),)
    size = dict(
        limit=20,
        flops=2 * count * Y * SLICE * SLICE * LANES,
        moved=count * Y * SLICE * SLICE * 2,
    )
    sent, rhs, *sums = call(
        functools.partial(send_kernel, stage),
        outs,
        [VMEM] * 5,
        *plan,
        tiles,
        slots,
        **size,
    )
    received = lax.ppermute(sent, "core", CORE_SWAP)
    given = [tiles, rhs] + (sums if stage == 1 else [])
    kept = call(functools.partial(keep_kernel, stage), slices, [VMEM] * len(given), *given, **size)
    parts = []
    for step in (3, 1, 2):
        part = kept[step] + received[step]
        if stage == 2:
            part = part.astype(BF16)
        parts.append(lax.ppermute(part, "y", [(y, (y + step) % Y) for y in range(Y)]))
    return (kept, received, *parts), sums


def added(refs):
    own, received, *parts = refs
    value = own[0] + received[0]
    for part in parts:
        value = value + part[...].astype(F32)
    return value


def first_kernel(*refs):
    vectors, first, payload = refs[-3:]
    value = added(refs[:-3])
    first[...] = value
    payload[:SLICE] = value.astype(BF16)
    wide = vectors[...].astype(F32)
    wide = jnp.sum(wide * wide, axis=0, keepdims=True)
    sums = jnp.concatenate([jnp.sum(value * value, axis=0, keepdims=True), wide], axis=0)
    payload[SLICE:] = pad_rows(split(sums), EXT).astype(BF16)


def second_kernel(*refs):
    payload, gathered = refs[-2:]
    value = added(refs[:-2])
    payload[:SLICE] = value[:SLICE].astype(BF16)
    sums = value[SLICE:]
    gathered[...] = sums
    payload[SLICE:] = pad_rows(split(sums[2:4]), EXT).astype(BF16)


def gram_kernel(*refs):
    first, sums, filtered, gram = refs[-4:]
    third = added(refs[:-4])
    totals = jnp.sum(sums[...], axis=1, keepdims=True)
    spread = totals[0:1] / totals[1:2]
    value = 4.0 * third - 3.0 * spread * first[...]
    filtered[...] = value
    full = lax.dot_general(
        value, value, (((0,), (0,)), ((), ())), precision=HIGHEST, preferred_element_type=F32
    )
    gram64 = full[:HALF, :HALF] + full[HALF:, HALF:]
    half = HALF // 2
    blocks = (gram64[:half, :half], gram64[half:, :half], gram64[half:, half:])
    gram[...] = jnp.concatenate(
        [
            jnp.concatenate([block[i : i + 8] for i in range(0, half, 8)], axis=1)
            for block in blocks
        ],
        axis=0,
    )


def inverse_factor(work):
    step = 8
    shape = (step, LANES)
    groups = [work[i : i + step] for i in range(0, HALF, step)]
    row = lax.broadcasted_iota(jnp.int32, shape, 0)
    for g in range(len(groups)):
        rest = range(g, len(groups))
        columns = [
            {h: jnp.broadcast_to(groups[h][:, step * g + j : step * g + j + 1], shape) for h in rest}
            for j in range(step)
        ]
        entries = [
            [jnp.broadcast_to(columns[j][g][i : i + 1], shape) for j in range(i + 1)] for i in range(step)
        ]
        rows = [jnp.broadcast_to(groups[g][i : i + 1], shape) for i in range(step)]
        pivots = entries[0][0]
        for j in range(step):
            pivot = entries[j][j]
            pivots = jnp.where(row == j, pivot, pivots)
            reciprocal = 1.0 / pivot
            scaled = rows[j] * reciprocal
            for i in range(j + 1, step):
                factor = entries[i][j] * reciprocal
                rows[i] = rows[i] - factor * rows[j]
                for m in range(j + 1, i + 1):
                    entries[i][m] = entries[i][m] - factor * entries[m][j]
                for h in rest:
                    columns[i][h] = columns[i][h] - factor * columns[j][h]
            for h in rest:
                column = columns[j][h]
                if h == g:
                    column = jnp.where(row > j, column, 0.0)
                groups[h] = groups[h] - column * scaled
        groups[g] = groups[g] / jnp.sqrt(pivots)
    return jnp.concatenate(groups, axis=0)


def finish_kernel(scale, grams, filtered, out):
    packed = grams[0]
    for i in range(1, grams.shape[0]):
        packed = packed + grams[i]
    half = HALF // 2
    top, corner, bottom = (
        jnp.concatenate([packed[b : b + 8, i : i + half] for i in range(0, LANES, half)], axis=0)
        for b in (0, 8, 16)
    )
    square = jnp.concatenate(
        [jnp.concatenate([top, corner.T], axis=1), jnp.concatenate([corner, bottom], axis=1)], axis=0
    )
    row = lax.broadcasted_iota(jnp.int32, (HALF, LANES), 0)
    lane = lax.broadcasted_iota(jnp.int32, (HALF, LANES), 1)
    unit = jnp.where(lane - HALF == row, 1.0, 0.0)
    work = jnp.where(lane < HALF, jnp.concatenate([square, square], axis=1), unit)
    inverse = inverse_factor(work)[:, HALF:] * scale
    for block in range(2):
        out[block] = lax.dot_general(
            inverse,
            filtered[:, block * HALF : (block + 1) * HALF],
            (((1,), (1,)), ((), ())),
            precision=HIGHEST,
            preferred_element_type=F32,
        )


def on_device(tiles, tile_row, tile_col, tile_count, block_vectors):
    blocks, rows, vectors = block_vectors.shape
    count = tiles.shape[0]
    plan = (tile_row, tile_col, tile_count)
    slice_shape, payload_shape = (rows, LANES), (rows + EXT, LANES)
    packed = block_vectors.transpose(0, 2, 1).reshape(blocks * vectors, rows)
    packed = call(turn_kernel, (slice_shape, BF16), [VMEM], packed)
    token = call(place_kernel, ((SUMS, LANES), F32), [VMEM], tiles, limit=20, moved=2 * tiles.size)
    parts, _ = apply_graph(0, plan, tiles, window(0, packed, *plan, token))
    first, payload = call(
        first_kernel,
        ((slice_shape, F32), (payload_shape, BF16)),
        [VMEM] * (len(parts) + 1),
        *parts,
        packed,
    )
    parts, _ = apply_graph(1, plan, tiles, window(1, payload))
    payload, gathered = call(
        second_kernel,
        ((payload_shape, BF16), ((SUMS, LANES), F32)),
        [VMEM] * len(parts),
        *parts,
    )
    parts, sums = apply_graph(2, plan, tiles, window(2, payload, gathered))
    filtered, gram = call(
        gram_kernel,
        ((slice_shape, F32), ((24, LANES), F32)),
        [VMEM] * (len(parts) + 2),
        *parts,
        first,
        *sums,
    )

    gram = gram + lax.ppermute(gram, "core", CORE_SWAP)
    grams = lax.all_to_all(jnp.broadcast_to(gram[None], (X * Y,) + gram.shape), ("x", "y"), 0, 0)
    gram = jnp.sum(grams, axis=0)
    grams = lax.all_to_all(jnp.broadcast_to(gram[None], (Z,) + gram.shape), "z", 0, 0)
    total_rows = blocks * rows * X * Z * Y * CORE
    out = call(
        functools.partial(finish_kernel, math.sqrt(total_rows)),
        ((blocks, vectors, rows), F32),
        [VMEM] * 2,
        grams,
        filtered,
    )
    return out.transpose(0, 2, 1)


def solution(mesh):
    grid = Mesh(mesh.devices.reshape(X, Z, Y, CORE), ALL)
    row, col = ("x", "z"), ("y", "core")
    in_specs = (P(row, None, col), P(row), P(row), P(row), P(row, col, None))
    return jax.shard_map(
        on_device, mesh=grid, in_specs=in_specs, out_specs=P(row, col, None), check_vma=False
    )
```

```python
import functools
import math

import jax
import jax.numpy as jnp
from jax import lax
from jax.experimental import pallas as pl
from jax.experimental.pallas import tpu as pltpu
from jax.sharding import Mesh, PartitionSpec as P

X, Z, Y, CORE = 4, 8, 4, 2
ALL = ("x", "z", "y", "core")
SLICE = 256
LANES = 128
HALF = LANES // 2
EXT = 16
SUMS = 8
CORE_SWAP = [(0, 1), (1, 0)]
HIGHEST = lax.Precision.HIGHEST
VMEM = pl.BlockSpec(memory_space=pltpu.VMEM)
SMEM = pl.BlockSpec(memory_space=pltpu.SMEM)
F32, BF16 = jnp.float32, jnp.bfloat16


def call(kernel, outs, specs, *args, scratch=(), limit=8, flops=0, moved=0):
    single = not isinstance(outs[0][0], tuple)
    shapes = (outs,) if single else outs
    result = pl.pallas_call(
        kernel,
        out_shape=tuple(jax.ShapeDtypeStruct(*s) for s in shapes),
        in_specs=specs,
        out_specs=(VMEM,) * len(shapes),
        scratch_shapes=scratch,
        compiler_params=pltpu.CompilerParams(vmem_limit_bytes=limit << 20),
        cost_estimate=pl.CostEstimate(flops=flops, bytes_accessed=moved, transcendentals=0),
    )(*args)
    return result[0] if single else result


def x_neighbour_pairs():
    pairs = []
    for x in range(X):
        for z in range(Z):
            to = (x + 1) % X if z >= Z // 2 else (x - 1) % X
            for c in range(Y * CORE):
                pairs.append(((x * Z + z) * Y * CORE + c, (to * Z + z) * Y * CORE + c))
    return pairs


def split(value):
    high = value.astype(BF16).astype(F32)
    rest = value - high
    middle = rest.astype(BF16).astype(F32)
    return jnp.concatenate([high, middle, rest - middle], axis=0)


def joined(rows):
    return rows[0:2] + rows[2:4] + rows[4:6]


def pad_rows(value, count):
    return jnp.concatenate([value, jnp.zeros((count - value.shape[0], LANES), F32)], axis=0)


def place_kernel(tiles, token):
    token[...] = jnp.zeros_like(token)


def turn_kernel(vectors, out):
    out[...] = vectors[...].astype(F32).T.astype(BF16)


def pieces_kernel(stage, own, other, *refs):
    out = refs[-1]
    z = lax.axis_index("z")
    half = Z // 2
    mine, theirs = own[:SLICE], other[:SLICE]
    for target in range(Z):
        use_other = jnp.where(z < half, z <= target - half - 1, z >= target + half)

        @pl.when(use_other)
        def _():
            out[target, :SLICE] = theirs

        @pl.when(jnp.logical_not(use_other))
        def _():
            out[target, :SLICE] = mine

    if stage == 0:
        return
    theirs = other[SLICE:].astype(F32)
    if stage == 1:
        mine = own[SLICE:].astype(F32)
        extra = pad_rows(jnp.concatenate([mine[:6], theirs[:6]], axis=0), EXT)
    else:
        extra = pad_rows(split(refs[0][0:2] + joined(theirs)), EXT)
    extra = extra.astype(BF16)
    for target in range(Z):
        out[target, SLICE:] = extra


def window(stage, own, *parts):
    other = lax.ppermute(own, ALL, x_neighbour_pairs())
    rows = SLICE if stage == 0 else SLICE + EXT
    pieces = call(
        functools.partial(pieces_kernel, stage),
        ((Z, rows, LANES), BF16),
        [VMEM] * (2 + len(parts)),
        own,
        other,
        *parts,
    )
    return lax.all_to_all(pieces, "z", 0, 0)


def multiply(core, tiles, rhs, out, sums):
    y = lax.axis_index("y")
    for i in range(Y):
        start = pl.multiple_of((lax.rem(y + i, Y) * CORE + core) * SLICE, SLICE)
        total = jnp.zeros((SLICE, LANES), F32)
        for t in range(tiles.shape[0]):
            total = total + jnp.dot(
                tiles[t, pl.ds(start, SLICE), :], rhs[t], preferred_element_type=F32
            )
        out[i, :SLICE] = total
        if sums is not None:
            out[i, SLICE:] = sums


def send_kernel(stage, tile_row, tile_col, tile_count, tiles, slots, out, rhs, *sums_ref):
    lane = lax.broadcasted_iota(jnp.int32, (SLICE, LANES), 1)
    for t in range(tiles.shape[0]):
        row, col = tile_row[t], tile_col[t]
        parity, slot = col & 1, lax.shift_right_logical(col, 1) & (Z - 1)
        live = t < tile_count[0]
        first = row * HALF
        vectors = slots[slot, :SLICE].astype(F32)
        other_half = pltpu.roll(vectors, HALF, axis=1)
        vectors = jnp.where(parity == row, vectors, other_half)
        keep = (lane >= first) & (lane < first + HALF) & live
        rhs[t] = jnp.where(keep, vectors, 0.0).astype(BF16)
    sums = None
    if stage:
        extra = [slots[z, SLICE:].astype(F32) for z in range(Z)]
    if stage == 1:
        low, high = sum(extra[: Z // 2]), sum(extra[Z // 2 :])
        own_low, own_high = joined(low), joined(high)
        next_low, next_high = joined(low[6:12]), joined(high[6:12])
        upper = lax.axis_index("z") >= Z // 2
        gathered = jnp.where(upper, own_high + next_high, own_low + next_low)
        passed = jnp.where(upper, next_high + own_low, next_low + own_high)
        sums = pad_rows(jnp.concatenate([gathered, passed], axis=0), SUMS)
        sums_ref[0][...] = sums
    if stage == 2:
        sums_ref[0][...] = pad_rows(joined(extra[0]) + joined(extra[Z // 2]), SUMS)
    multiply(1 - lax.axis_index("core"), tiles, rhs, out, sums)


def keep_kernel(stage, tiles, rhs, *refs):
    sums = refs[0][...] if stage == 1 else None
    multiply(lax.axis_index("core"), tiles, rhs, refs[-1], sums)


def apply_graph(stage, plan, tiles, slots):
    count = tiles.shape[0]
    rows = SLICE + (SUMS if stage == 1 else 0)
    slices = ((Y, rows, LANES), F32)
    outs = (slices, ((count, SLICE, LANES), BF16))
    if stage:
        outs += (((SUMS, LANES), F32),)
    size = dict(
        limit=20,
        flops=2 * count * Y * SLICE * SLICE * LANES,
        moved=count * Y * SLICE * SLICE * 2,
    )
    sent, rhs, *sums = call(
        functools.partial(send_kernel, stage),
        outs,
        [VMEM] * 5,
        *plan,
        tiles,
        slots,
        **size,
    )
    received = lax.ppermute(sent, "core", CORE_SWAP)
    given = [tiles, rhs] + (sums if stage == 1 else [])
    kept = call(functools.partial(keep_kernel, stage), slices, [VMEM] * len(given), *given, **size)
    parts = []
    for step in (2, 3, 1):
        part = kept[step] + received[step]
        if stage == 2:
            part = part.astype(BF16)
        parts.append(lax.ppermute(part, "y", [(y, (y + step) % Y) for y in range(Y)]))
    return (kept, received, *parts), sums


def added(refs):
    own, received, *parts = refs
    value = own[0] + received[0]
    for part in parts:
        value = value + part[...].astype(F32)
    return value


def first_kernel(*refs):
    vectors, first, payload = refs[-3:]
    value = added(refs[:-3])
    first[...] = value
    payload[:SLICE] = value.astype(BF16)
    wide = vectors[...].astype(F32)
    wide = jnp.sum(wide * wide, axis=0, keepdims=True)
    sums = jnp.concatenate([jnp.sum(value * value, axis=0, keepdims=True), wide], axis=0)
    payload[SLICE:] = pad_rows(split(sums), EXT).astype(BF16)


def second_kernel(*refs):
    payload, gathered = refs[-2:]
    value = added(refs[:-2])
    payload[:SLICE] = value[:SLICE].astype(BF16)
    sums = value[SLICE:]
    gathered[...] = sums
    payload[SLICE:] = pad_rows(split(sums[2:4]), EXT).astype(BF16)


def gram_kernel(*refs):
    first, sums, filtered, gram = refs[-4:]
    third = added(refs[:-4])
    totals = jnp.sum(sums[...], axis=1, keepdims=True)
    spread = totals[0:1] / totals[1:2]
    value = 4.0 * third - 3.0 * spread * first[...]
    filtered[...] = value
    full = lax.dot_general(
        value, value, (((0,), (0,)), ((), ())), precision=HIGHEST, preferred_element_type=F32
    )
    gram64 = full[:HALF, :HALF] + full[HALF:, HALF:]
    half = HALF // 2
    blocks = (gram64[:half, :half], gram64[half:, :half], gram64[half:, half:])
    gram[...] = jnp.concatenate(
        [
            jnp.concatenate([block[i : i + 8] for i in range(0, half, 8)], axis=1)
            for block in blocks
        ],
        axis=0,
    )


def inverse_factor(work):
    step = 8
    shape = (step, LANES)
    groups = [work[i : i + step] for i in range(0, HALF, step)]
    row = lax.broadcasted_iota(jnp.int32, shape, 0)
    for g in range(len(groups)):
        rest = range(g, len(groups))
        columns = [
            {h: jnp.broadcast_to(groups[h][:, step * g + j : step * g + j + 1], shape) for h in rest}
            for j in range(step)
        ]
        entries = [
            [jnp.broadcast_to(columns[j][g][i : i + 1], shape) for j in range(i + 1)] for i in range(step)
        ]
        rows = [jnp.broadcast_to(groups[g][i : i + 1], shape) for i in range(step)]
        pivots = entries[0][0]
        for j in range(step):
            pivot = entries[j][j]
            pivots = jnp.where(row == j, pivot, pivots)
            reciprocal = 1.0 / pivot
            scaled = rows[j] * reciprocal
            for i in range(j + 1, step):
                factor = entries[i][j] * reciprocal
                rows[i] = rows[i] - factor * rows[j]
                for m in range(j + 1, i + 1):
                    entries[i][m] = entries[i][m] - factor * entries[m][j]
                for h in rest:
                    columns[i][h] = columns[i][h] - factor * columns[j][h]
            for h in rest:
                column = columns[j][h]
                if h == g:
                    column = jnp.where(row > j, column, 0.0)
                groups[h] = groups[h] - column * scaled
        groups[g] = groups[g] / jnp.sqrt(pivots)
    return jnp.concatenate(groups, axis=0)


def finish_kernel(scale, grams, filtered, out):
    packed = grams[0]
    for i in range(1, grams.shape[0]):
        packed = packed + grams[i]
    half = HALF // 2
    top, corner, bottom = (
        jnp.concatenate([packed[b : b + 8, i : i + half] for i in range(0, LANES, half)], axis=0)
        for b in (0, 8, 16)
    )
    square = jnp.concatenate(
        [jnp.concatenate([top, corner.T], axis=1), jnp.concatenate([corner, bottom], axis=1)], axis=0
    )
    row = lax.broadcasted_iota(jnp.int32, (HALF, LANES), 0)
    lane = lax.broadcasted_iota(jnp.int32, (HALF, LANES), 1)
    unit = jnp.where(lane - HALF == row, 1.0, 0.0)
    work = jnp.where(lane < HALF, jnp.concatenate([square, square], axis=1), unit)
    inverse = inverse_factor(work)[:, HALF:] * scale
    for block in range(2):
        out[block] = lax.dot_general(
            inverse,
            filtered[:, block * HALF : (block + 1) * HALF],
            (((1,), (1,)), ((), ())),
            precision=HIGHEST,
            preferred_element_type=F32,
        )


def on_device(tiles, tile_row, tile_col, tile_count, block_vectors):
    blocks, rows, vectors = block_vectors.shape
    count = tiles.shape[0]
    plan = (tile_row, tile_col, tile_count)
    slice_shape, payload_shape = (rows, LANES), (rows + EXT, LANES)
    packed = block_vectors.transpose(0, 2, 1).reshape(blocks * vectors, rows)
    packed = call(turn_kernel, (slice_shape, BF16), [VMEM], packed)
    token = call(place_kernel, ((SUMS, LANES), F32), [VMEM], tiles, limit=20, moved=2 * tiles.size)
    parts, _ = apply_graph(0, plan, tiles, window(0, packed, *plan, token))
    first, payload = call(
        first_kernel,
        ((slice_shape, F32), (payload_shape, BF16)),
        [VMEM] * (len(parts) + 1),
        *parts,
        packed,
    )
    parts, _ = apply_graph(1, plan, tiles, window(1, payload))
    payload, gathered = call(
        second_kernel,
        ((payload_shape, BF16), ((SUMS, LANES), F32)),
        [VMEM] * len(parts),
        *parts,
    )
    parts, sums = apply_graph(2, plan, tiles, window(2, payload, gathered))
    filtered, gram = call(
        gram_kernel,
        ((slice_shape, F32), ((24, LANES), F32)),
        [VMEM] * (len(parts) + 2),
        *parts,
        first,
        *sums,
    )

    gram = gram + lax.ppermute(gram, "core", CORE_SWAP)
    grams = lax.all_to_all(jnp.broadcast_to(gram[None], (X * Y,) + gram.shape), ("x", "y"), 0, 0)
    gram = jnp.sum(grams, axis=0)
    grams = lax.all_to_all(jnp.broadcast_to(gram[None], (Z,) + gram.shape), "z", 0, 0)
    total_rows = blocks * rows * X * Z * Y * CORE
    out = call(
        functools.partial(finish_kernel, math.sqrt(total_rows)),
        ((blocks, vectors, rows), F32),
        [VMEM] * 2,
        grams,
        filtered,
    )
    return out.transpose(0, 2, 1)


def solution(mesh):
    grid = Mesh(mesh.devices.reshape(X, Z, Y, CORE), ALL)
    row, col = ("x", "z"), ("y", "core")
    in_specs = (P(row, None, col), P(row), P(row), P(row), P(row, col, None))
    return jax.shard_map(
        on_device, mesh=grid, in_specs=in_specs, out_specs=P(row, col, None), check_vma=False
    )
```

```python
import functools
import math

import jax
import jax.numpy as jnp
from jax import lax
from jax.experimental import pallas as pl
from jax.experimental.pallas import tpu as pltpu
from jax.sharding import Mesh, PartitionSpec as P

X, Z, Y, CORE = 4, 8, 4, 2
ALL = ("x", "z", "y", "core")
SLICE = 256
LANES = 128
HALF = LANES // 2
EXT = 16
SUMS = 8
CORE_SWAP = [(0, 1), (1, 0)]
HIGHEST = lax.Precision.HIGHEST
VMEM = pl.BlockSpec(memory_space=pltpu.VMEM)
SMEM = pl.BlockSpec(memory_space=pltpu.SMEM)
F32, BF16 = jnp.float32, jnp.bfloat16


def call(kernel, outs, specs, *args, scratch=(), limit=8, flops=0, moved=0):
    single = not isinstance(outs[0][0], tuple)
    shapes = (outs,) if single else outs
    result = pl.pallas_call(
        kernel,
        out_shape=tuple(jax.ShapeDtypeStruct(*s) for s in shapes),
        in_specs=specs,
        out_specs=(VMEM,) * len(shapes),
        scratch_shapes=scratch,
        compiler_params=pltpu.CompilerParams(vmem_limit_bytes=limit << 20),
        cost_estimate=pl.CostEstimate(flops=flops, bytes_accessed=moved, transcendentals=0),
    )(*args)
    return result[0] if single else result


def x_neighbour_pairs():
    pairs = []
    for x in range(X):
        for z in range(Z):
            to = (x + 1) % X if z >= Z // 2 else (x - 1) % X
            for c in range(Y * CORE):
                pairs.append(((x * Z + z) * Y * CORE + c, (to * Z + z) * Y * CORE + c))
    return pairs


def split(value):
    high = value.astype(BF16).astype(F32)
    rest = value - high
    middle = rest.astype(BF16).astype(F32)
    return jnp.concatenate([high, middle, rest - middle], axis=0)


def joined(rows):
    return rows[0:2] + rows[2:4] + rows[4:6]


def pad_rows(value, count):
    return jnp.concatenate([value, jnp.zeros((count - value.shape[0], LANES), F32)], axis=0)


def place_kernel(tiles, token):
    token[...] = jnp.zeros_like(token)


def turn_kernel(vectors, out):
    out[...] = vectors[...].astype(F32).T.astype(BF16)


def pieces_kernel(stage, own, other, *refs):
    out = refs[-1]
    z = lax.axis_index("z")
    half = Z // 2
    mine, theirs = own[:SLICE], other[:SLICE]
    for target in range(Z):
        use_other = jnp.where(z < half, z <= target - half - 1, z >= target + half)

        @pl.when(use_other)
        def _():
            out[target, :SLICE] = theirs

        @pl.when(jnp.logical_not(use_other))
        def _():
            out[target, :SLICE] = mine

    if stage == 0:
        return
    theirs = other[SLICE:].astype(F32)
    if stage == 1:
        mine = own[SLICE:].astype(F32)
        extra = pad_rows(jnp.concatenate([mine[:6], theirs[:6]], axis=0), EXT)
    else:
        extra = pad_rows(split(refs[0][0:2] + joined(theirs)), EXT)
    extra = extra.astype(BF16)
    for target in range(Z):
        out[target, SLICE:] = extra


def window(stage, own, *parts):
    other = lax.ppermute(own, ALL, x_neighbour_pairs())
    rows = SLICE if stage == 0 else SLICE + EXT
    pieces = call(
        functools.partial(pieces_kernel, stage),
        ((Z, rows, LANES), BF16),
        [VMEM] * (2 + len(parts)),
        own,
        other,
        *parts,
    )
    return lax.all_to_all(pieces, "z", 0, 0)


def multiply(core, tiles, rhs, out, sums):
    y = lax.axis_index("y")
    for i in range(Y):
        start = pl.multiple_of((lax.rem(y + i, Y) * CORE + core) * SLICE, SLICE)
        total = jnp.zeros((SLICE, LANES), F32)
        for t in range(tiles.shape[0]):
            total = total + jnp.dot(
                tiles[t, pl.ds(start, SLICE), :], rhs[t], preferred_element_type=F32
            )
        out[i, :SLICE] = total
        if sums is not None:
            out[i, SLICE:] = sums


def send_kernel(stage, tile_row, tile_col, tile_count, tiles, slots, out, rhs, *sums_ref):
    lane = lax.broadcasted_iota(jnp.int32, (SLICE, LANES), 1)
    for t in range(tiles.shape[0]):
        row, col = tile_row[t], tile_col[t]
        parity, slot = col & 1, lax.shift_right_logical(col, 1) & (Z - 1)
        live = t < tile_count[0]
        first = row * HALF
        vectors = slots[slot, :SLICE].astype(F32)
        other_half = pltpu.roll(vectors, HALF, axis=1)
        vectors = jnp.where(parity == row, vectors, other_half)
        keep = (lane >= first) & (lane < first + HALF) & live
        rhs[t] = jnp.where(keep, vectors, 0.0).astype(BF16)
    sums = None
    if stage:
        extra = [slots[z, SLICE:].astype(F32) for z in range(Z)]
    if stage == 1:
        low, high = sum(extra[: Z // 2]), sum(extra[Z // 2 :])
        own_low, own_high = joined(low), joined(high)
        next_low, next_high = joined(low[6:12]), joined(high[6:12])
        upper = lax.axis_index("z") >= Z // 2
        gathered = jnp.where(upper, own_high + next_high, own_low + next_low)
        passed = jnp.where(upper, next_high + own_low, next_low + own_high)
        sums = pad_rows(jnp.concatenate([gathered, passed], axis=0), SUMS)
        sums_ref[0][...] = sums
    if stage == 2:
        sums_ref[0][...] = pad_rows(joined(extra[0]) + joined(extra[Z // 2]), SUMS)
    multiply(1 - lax.axis_index("core"), tiles, rhs, out, sums)


def keep_kernel(stage, tiles, rhs, *refs):
    sums = refs[0][...] if stage == 1 else None
    multiply(lax.axis_index("core"), tiles, rhs, refs[-1], sums)


def apply_graph(stage, plan, tiles, slots):
    count = tiles.shape[0]
    rows = SLICE + (SUMS if stage == 1 else 0)
    slices = ((Y, rows, LANES), F32)
    outs = (slices, ((count, SLICE, LANES), BF16))
    if stage:
        outs += (((SUMS, LANES), F32),)
    size = dict(
        limit=20,
        flops=2 * count * Y * SLICE * SLICE * LANES,
        moved=count * Y * SLICE * SLICE * 2,
    )
    sent, rhs, *sums = call(
        functools.partial(send_kernel, stage),
        outs,
        [VMEM] * 5,
        *plan,
        tiles,
        slots,
        **size,
    )
    received = lax.ppermute(sent, "core", CORE_SWAP)
    given = [tiles, rhs] + (sums if stage == 1 else [])
    kept = call(functools.partial(keep_kernel, stage), slices, [VMEM] * len(given), *given, **size)
    parts = []
    for step in (2, 3, 1):
        part = kept[step] + received[step]
        if stage == 2:
            part = part.astype(BF16)
        parts.append(lax.ppermute(part, "y", [(y, (y + step) % Y) for y in range(Y)]))
    return (kept, received, *parts), sums


def added(refs):
    own, received, *parts = refs
    value = own[0] + received[0]
    for part in parts:
        value = value + part[...].astype(F32)
    return value


def first_kernel(*refs):
    vectors, first, payload = refs[-3:]
    value = added(refs[:-3])
    first[...] = value
    payload[:SLICE] = value.astype(BF16)
    wide = vectors[...].astype(F32)
    wide = jnp.sum(wide * wide, axis=0, keepdims=True)
    sums = jnp.concatenate([jnp.sum(value * value, axis=0, keepdims=True), wide], axis=0)
    payload[SLICE:] = pad_rows(split(sums), EXT).astype(BF16)


def second_kernel(*refs):
    payload, gathered = refs[-2:]
    value = added(refs[:-2])
    payload[:SLICE] = value[:SLICE].astype(BF16)
    sums = value[SLICE:]
    gathered[...] = sums
    payload[SLICE:] = pad_rows(split(sums[2:4]), EXT).astype(BF16)


def gram_kernel(*refs):
    first, sums, filtered, gram = refs[-4:]
    third = added(refs[:-4])
    totals = jnp.sum(sums[...], axis=1, keepdims=True)
    spread = totals[0:1] / totals[1:2]
    value = 4.0 * third - 3.0 * spread * first[...]
    filtered[...] = value
    full = lax.dot_general(
        value, value, (((0,), (0,)), ((), ())), precision=HIGHEST, preferred_element_type=F32
    )
    gram64 = full[:HALF, :HALF] + full[HALF:, HALF:]
    half = HALF // 2
    blocks = (gram64[:half, :half], gram64[half:, :half], gram64[half:, half:])
    gram[...] = jnp.concatenate(
        [
            jnp.concatenate([block[i : i + 8] for i in range(0, half, 8)], axis=1)
            for block in blocks
        ],
        axis=0,
    )


def inverse_factor(work):
    step = 8
    shape = (step, LANES)
    groups = [work[i : i + step] for i in range(0, HALF, step)]
    row = lax.broadcasted_iota(jnp.int32, shape, 0)
    for g in range(len(groups)):
        rest = range(g, len(groups))
        columns = [
            {h: jnp.broadcast_to(groups[h][:, step * g + j : step * g + j + 1], shape) for h in rest}
            for j in range(step)
        ]
        entries = [
            [jnp.broadcast_to(columns[j][g][i : i + 1], shape) for j in range(i + 1)] for i in range(step)
        ]
        rows = [jnp.broadcast_to(groups[g][i : i + 1], shape) for i in range(step)]
        pivots = entries[0][0]
        for j in range(step):
            pivot = entries[j][j]
            pivots = jnp.where(row == j, pivot, pivots)
            reciprocal = 1.0 / pivot
            scaled = rows[j] * reciprocal
            for i in range(j + 1, step):
                factor = entries[i][j] * reciprocal
                rows[i] = rows[i] - factor * rows[j]
                for m in range(j + 1, i + 1):
                    entries[i][m] = entries[i][m] - factor * entries[m][j]
                for h in rest:
                    columns[i][h] = columns[i][h] - factor * columns[j][h]
            for h in rest:
                column = columns[j][h]
                if h == g:
                    column = jnp.where(row > j, column, 0.0)
                groups[h] = groups[h] - column * scaled
        groups[g] = groups[g] / jnp.sqrt(pivots)
    return jnp.concatenate(groups, axis=0)


def finish_kernel(scale, grams, filtered, out):
    packed = grams[0]
    for i in range(1, grams.shape[0]):
        packed = packed + grams[i]
    half = HALF // 2
    top, corner, bottom = (
        jnp.concatenate([packed[b : b + 8, i : i + half] for i in range(0, LANES, half)], axis=0)
        for b in (0, 8, 16)
    )
    square = jnp.concatenate(
        [jnp.concatenate([top, corner.T], axis=1), jnp.concatenate([corner, bottom], axis=1)], axis=0
    )
    row = lax.broadcasted_iota(jnp.int32, (HALF, LANES), 0)
    lane = lax.broadcasted_iota(jnp.int32, (HALF, LANES), 1)
    unit = jnp.where(lane - HALF == row, 1.0, 0.0)
    work = jnp.where(lane < HALF, jnp.concatenate([square, square], axis=1), unit)
    inverse = inverse_factor(work)[:, HALF:] * scale
    rows = filtered.shape[0]
    both = jnp.concatenate([filtered[:, :HALF], filtered[:, HALF:]], axis=0)
    basis = lax.dot_general(
        inverse, both, (((1,), (1,)), ((), ())), precision=HIGHEST, preferred_element_type=F32
    )
    out[0], out[1] = basis[:, :rows], basis[:, rows:]


def on_device(tiles, tile_row, tile_col, tile_count, block_vectors):
    blocks, rows, vectors = block_vectors.shape
    count = tiles.shape[0]
    plan = (tile_row, tile_col, tile_count)
    slice_shape, payload_shape = (rows, LANES), (rows + EXT, LANES)
    packed = block_vectors.transpose(0, 2, 1).reshape(blocks * vectors, rows)
    packed = call(turn_kernel, (slice_shape, BF16), [VMEM], packed)
    token = call(place_kernel, ((SUMS, LANES), F32), [VMEM], tiles, limit=20, moved=2 * tiles.size)
    parts, _ = apply_graph(0, plan, tiles, window(0, packed, *plan, token))
    first, payload = call(
        first_kernel,
        ((slice_shape, F32), (payload_shape, BF16)),
        [VMEM] * (len(parts) + 1),
        *parts,
        packed,
    )
    parts, _ = apply_graph(1, plan, tiles, window(1, payload))
    payload, gathered = call(
        second_kernel,
        ((payload_shape, BF16), ((SUMS, LANES), F32)),
        [VMEM] * len(parts),
        *parts,
    )
    parts, sums = apply_graph(2, plan, tiles, window(2, payload, gathered))
    filtered, gram = call(
        gram_kernel,
        ((slice_shape, F32), ((24, LANES), F32)),
        [VMEM] * (len(parts) + 2),
        *parts,
        first,
        *sums,
    )

    gram = gram + lax.ppermute(gram, "core", CORE_SWAP)
    grams = lax.all_to_all(jnp.broadcast_to(gram[None], (X * Y,) + gram.shape), ("x", "y"), 0, 0)
    gram = jnp.sum(grams, axis=0)
    grams = lax.all_to_all(jnp.broadcast_to(gram[None], (Z,) + gram.shape), "z", 0, 0)
    total_rows = blocks * rows * X * Z * Y * CORE
    out = call(
        functools.partial(finish_kernel, math.sqrt(total_rows)),
        ((blocks, vectors, rows), F32),
        [VMEM] * 2,
        grams,
        filtered,
    )
    return out.transpose(0, 2, 1)


def solution(mesh):
    grid = Mesh(mesh.devices.reshape(X, Z, Y, CORE), ALL)
    row, col = ("x", "z"), ("y", "core")
    in_specs = (P(row, None, col), P(row), P(row), P(row), P(row, col, None))
    return jax.shard_map(
        on_device, mesh=grid, in_specs=in_specs, out_specs=P(row, col, None), check_vma=False
    )
```
